256 devices in a mesh: grp: 16 (over z, core), sp: 16 (over x, y).
Axes of the slice: x: 4, y: 4, z: 8, core: 2. Of those that a mesh axis runs over, the one named last changes fastest.
Arguments:
- query: bfloat16 [32768, 4096], P(('grp', 'sp')), may hold values from -6 to 6
- key_value: bfloat16 [2, 32768, 512], P(None, ('grp', 'sp')), may hold values from -6 to 6
- grad_out: bfloat16 [32768, 4096], P(('grp', 'sp')), may hold values from -6 to 6
- segment_ids: int32 [16, 1, 2048], P('grp'), may hold values from 0 to 15, never falling along the last dimension, each value on 1 to 256 neighbouring positions
- lag: int32 [16, 1, 16], P('grp'), may hold values from 0 to 8
- q_gain: float32 [128], replicated, may hold values from 0.25 to 1.75
- k_gain: float32 [128], replicated, may hold values from 0.25 to 1.75
Outputs:
- attn_out: bfloat16 [32768, 4096], P(('grp', 'sp'))
- d_query: bfloat16 [32768, 4096], P(('grp', 'sp'))
- d_key_value: bfloat16 [2, 32768, 512], P(None, ('grp', 'sp'))
- d_q_gain: float32 [128], replicated
- d_k_gain: float32 [128], replicated
The draws below stay inside these ranges and needn't reach their ends.
Inputs may be any that keep to these rules, and one draw needn't show every extreme that they name: `segment_ids`: segment ids never fall along a sequence; every response of 0 to 15 has 1 to 256 tokens in each sequence, one exactly 256.
All inputs are finite; a program needn't handle non-finite values.
Results may differ from the reference program's by a relative error of at most 0.019.
Values may be sent and summed in bfloat16 or wider, within the bound.
No kernel may reach another device: no remote copies, remote signals or barrier semaphores. Data moves between devices by JAX's collectives and lax.ppermute only.
A program may use at most 128 MiB of HBM per device.

```python
import math
import jax
import jax.numpy as jnp
import numpy as np
from jax import lax

HEAD_SIZE = 128
HQ = 32
KEY_VALUE_HEADS = 4
RESP = 16
SEQS = 1
PACKED_TOKENS = 2048
TOKENS = 32768
N_GRP = 16
N_SP = 16


def set_ends(result, stream_key, smallest, top_value):
    dims = result.shape
    spot = [jax.random.randint(jax.random.fold_in(stream_key, axis), (), 0, dims[axis]) for axis in range(len(dims))]
    result = result.at[tuple(spot)].set(smallest)
    longest = dims.index(max(dims))
    spot[longest] = (spot[longest] + 1) % dims[longest]
    return result.at[tuple(spot)].set(top_value)


def level_of(rng, shape, cuts, smallest, top_value):
    def one(axis_at, parts):
        heights = jax.random.uniform(jax.random.fold_in(jax.random.fold_in(rng, 6), axis_at), (parts,), jnp.float32, smallest / len(cuts), top_value / len(cuts))
        return jnp.repeat(jnp.exp(heights), shape[axis_at] // parts).reshape((-1,) + (1,) * (len(shape) - axis_at - 1))

    level = one(*cuts[0])
    for cut in cuts[1:]:
        level = level * one(*cut)
    return level


def split_up(count, total, reach, skew):
    portions = [(1 << 20) // math.isqrt(rank ** skew) + 1 for rank in range(2, count + 1)]
    surplus, given = total - reach - (count - 1), [1] * (count - 1)
    while surplus > 0:
        movable = [i for i in range(count - 1) if given[i] < reach]
        whole, left = sum([portions[i] for i in movable]), surplus
        for i in movable:
            extra = min(reach - given[i], max(1, left * portions[i] // whole), surplus)
            given[i] = given[i] + extra
            surplus = surplus - extra
    return np.array([reach] + given)


def ragged(own_key, count, total, reach, skew):
    if count == 2:
        one = jax.random.randint(own_key, (), max(1, total - reach), min(reach, total - 1) + 1)
        return jnp.stack([one, total - one])
    tallies = jnp.asarray(split_up(count, total, reach, skew), jnp.int32)
    pairs = (count - 1) // 2
    source_of, taker = tallies[1:1 + 2 * pairs:2], tallies[2:2 + 2 * pairs:2]
    margin = jnp.minimum(source_of - 1, reach - taker)
    shifted = jax.random.randint(jax.random.fold_in(own_key, 1), (pairs,), 0, 1 << 20) % (margin + 1)
    tallies = tallies.at[1:1 + 2 * pairs:2].set(source_of - shifted).at[2:2 + 2 * pairs:2].set(taker + shifted)
    return tallies[jax.random.permutation(jax.random.fold_in(own_key, 2), count)]


def noise(rng, dims, deviation, most, shards=(), kind=jnp.bfloat16):
    factor_of = level_of(rng, dims, shards, -0.22, 0.18) if shards else 1.0
    result = jax.random.normal(rng, dims, jnp.float32) * deviation * factor_of
    return jnp.minimum(jnp.maximum(result, -most), most).astype(kind)


def setup_inputs(seed: int = 0) -> dict:
    key_list = jax.random.split(jax.random.key(seed), 8)
    return {
        "query": noise(key_list[0], (TOKENS, HQ * HEAD_SIZE), 1.0, 6.0, ((0, 256),)),
        "key_value": noise(key_list[1], (2, TOKENS, KEY_VALUE_HEADS * HEAD_SIZE), 1.0, 6.0, ((1, 256),)),
        "grad_out": noise(key_list[2], (TOKENS, HQ * HEAD_SIZE), 1.0, 6.0, ((0, 256),)),
        "segment_ids": jax.vmap(lambda own: jnp.searchsorted(jnp.cumsum(ragged(own, RESP, PACKED_TOKENS, 2 * PACKED_TOKENS // RESP, 2)), jnp.arange(PACKED_TOKENS), side="right"))(jax.random.split(key_list[3], N_GRP * SEQS)).reshape((N_GRP, SEQS, PACKED_TOKENS)).astype(jnp.int32),
        "lag": set_ends(jax.random.randint(key_list[4], (N_GRP, SEQS, RESP), 0, 9), jax.random.fold_in(key_list[4], 1), 0, 8).astype(jnp.int32),
        "q_gain": jnp.clip(1.0 + 0.15 * jax.random.normal(key_list[5], (HEAD_SIZE,), jnp.float32), 0.25, 1.75),
        "k_gain": jnp.clip(1.0 + 0.15 * jax.random.normal(key_list[6], (HEAD_SIZE,), jnp.float32), 0.25, 1.75),
    }


EPS = 1e-06

def rms_parts(x):
    inverse_root_scale = lax.rsqrt(lax.optimization_barrier(jnp.mean(x * x, -1, keepdims=True)) + EPS)
    return (x * inverse_root_scale, inverse_root_scale)

def norm_backward_pass(upstream_gradient, normalized_input, inverse_root_scale, norm_weight):
    scaled_input = upstream_gradient * norm_weight
    return inverse_root_scale * (scaled_input - normalized_input * lax.optimization_barrier(jnp.mean(scaled_input * normalized_input, -1, keepdims=True)))

def one_group(inputs, q_gain, k_gain):
    query, key_value, grad_out, segs, lagrow = inputs
    group_size = HQ // KEY_VALUE_HEADS
    per_dev = HQ // N_SP
    scale = HEAD_SIZE ** (-0.5)
    qhat, qrstd = rms_parts(query.astype(jnp.float32).reshape(PACKED_TOKENS, HQ, HEAD_SIZE))
    khat, krstd = rms_parts(key_value[0].astype(jnp.float32).reshape(PACKED_TOKENS, KEY_VALUE_HEADS, HEAD_SIZE))
    qn = (qhat * q_gain).astype(jnp.bfloat16)
    kn = (khat * k_gain).astype(jnp.bfloat16)
    values = key_value[1].reshape(PACKED_TOKENS, KEY_VALUE_HEADS, HEAD_SIZE)
    onehot = (segs[:, None] == jnp.arange(RESP, dtype=jnp.int32)[None, :]).astype(jnp.float32)
    coef = 8.0 / (8.0 + lagrow.astype(jnp.float32))
    token_coef = lax.optimization_barrier(jnp.sum(onehot * coef[None, :], 1))
    scaled_grad = (grad_out.astype(jnp.float32) * token_coef[:, None]).astype(jnp.bfloat16).reshape(PACKED_TOKENS, HQ, HEAD_SIZE)
    positions = jnp.arange(PACKED_TOKENS, dtype=jnp.int32)
    allowed = (positions[None, :] <= positions[:, None]) & (segs[None, :] == segs[:, None])

    def head_group(index):
        qgrp = lax.dynamic_slice_in_dim(qn, index * group_size, group_size, 1).astype(jnp.float32)
        dgrp = lax.dynamic_slice_in_dim(scaled_grad, index * group_size, group_size, 1).astype(jnp.float32)
        keys = lax.dynamic_index_in_dim(kn, index, 1, keepdims=False).astype(jnp.float32)
        vals = lax.dynamic_index_in_dim(values, index, 1, keepdims=False).astype(jnp.float32)
        scores = jnp.einsum('qgd,kd->gqk', qgrp, keys) * scale
        scores = jnp.where(allowed[None], scores, -jnp.inf)
        prob = jax.nn.softmax(scores, -1)
        pround = prob.astype(jnp.bfloat16)
        outb = jnp.einsum('gqk,kd->qgd', pround.astype(jnp.float32), vals).astype(jnp.bfloat16)
        delta = lax.optimization_barrier(jnp.sum(dgrp * outb.astype(jnp.float32), -1))
        dprob = jnp.einsum('qgd,kd->gqk', dgrp, vals)
        dsb = (prob * (dprob - delta.T[:, :, None]) * scale).astype(jnp.bfloat16).astype(jnp.float32)
        dqn = jnp.einsum('gqk,kd->qgd', dsb, keys).astype(jnp.bfloat16)
        dkh = jnp.einsum('gqk,qgd->gkd', dsb, qgrp)
        dvh = jnp.einsum('gqk,qgd->gkd', pround.astype(jnp.float32), dgrp)
        dkh = dkh.reshape(group_size // per_dev, per_dev, PACKED_TOKENS, HEAD_SIZE).sum(1).astype(jnp.bfloat16).astype(jnp.float32).sum(0)
        dvh = dvh.reshape(group_size // per_dev, per_dev, PACKED_TOKENS, HEAD_SIZE).sum(1).astype(jnp.bfloat16).astype(jnp.float32).sum(0)
        return (outb, dqn, dkh, dvh)
    outb, dqn, dkn, value_normed_gradient = lax.map(head_group, jnp.arange(KEY_VALUE_HEADS, dtype=jnp.int32))
    attn = jnp.transpose(outb, (1, 0, 2, 3)).reshape(PACKED_TOKENS, HQ * HEAD_SIZE)
    dqf = jnp.transpose(dqn, (1, 0, 2, 3)).reshape(PACKED_TOKENS, HQ, HEAD_SIZE).astype(jnp.float32)
    dkf = jnp.transpose(dkn, (1, 0, 2))
    value_flat_gradient = jnp.transpose(value_normed_gradient, (1, 0, 2)).reshape(PACKED_TOKENS, KEY_VALUE_HEADS * HEAD_SIZE)
    d_query = norm_backward_pass(dqf, qhat, qrstd, q_gain).astype(jnp.bfloat16).reshape(PACKED_TOKENS, HQ * HEAD_SIZE)
    key_gradient = norm_backward_pass(dkf, khat, krstd, k_gain).astype(jnp.bfloat16).reshape(PACKED_TOKENS, KEY_VALUE_HEADS * HEAD_SIZE)
    key_value_gradient = jnp.stack([key_gradient, value_flat_gradient.astype(jnp.bfloat16)])
    gq = lax.optimization_barrier(jnp.sum(dqf * qhat, (0, 1)))
    gk = lax.optimization_barrier(jnp.sum(dkf * khat, (0, 1)))
    return (attn, d_query, key_value_gradient, gq, gk)

def reference(query, key_value, grad_out, segment_ids, lag, q_gain, k_gain):
    count_all = N_GRP * SEQS
    inputs = (query.reshape(count_all, PACKED_TOKENS, HQ * HEAD_SIZE), jnp.transpose(key_value.reshape(2, count_all, PACKED_TOKENS, KEY_VALUE_HEADS * HEAD_SIZE), (1, 0, 2, 3)), grad_out.reshape(count_all, PACKED_TOKENS, HQ * HEAD_SIZE), segment_ids.reshape(count_all, PACKED_TOKENS), lag.reshape(count_all, RESP))
    attn, d_query, key_value_gradient, gq, gk = lax.map(lambda item: one_group(item, q_gain, k_gain), inputs)
    attn = attn.reshape(TOKENS, HQ * HEAD_SIZE)
    d_query = d_query.reshape(TOKENS, HQ * HEAD_SIZE)
    key_value_gradient = jnp.transpose(key_value_gradient, (1, 0, 2, 3)).reshape(2, TOKENS, KEY_VALUE_HEADS * HEAD_SIZE)
    return (attn, d_query, key_value_gradient, lax.optimization_barrier(jnp.sum(gq, 0)), lax.optimization_barrier(jnp.sum(gk, 0)))
```

```python
import functools
import math

import jax
import jax.numpy as jnp
from jax import lax
from jax.experimental import pallas as pl
from jax.experimental.pallas import tpu as pltpu
from jax.sharding import Mesh, PartitionSpec as P

EPS = 1e-06
LOG2E = math.log2(math.e)
ROWS = (((0,), (0,)), ((), ()))
LAST = (((1,), (1,)), ((), ()))
MIB = 2**20


def rms_parts(x):
    inverse = lax.rsqrt(jnp.mean(x * x, -1, keepdims=True) + EPS)
    return x * inverse, inverse


def attention_kernel(
    axis, q_ref, g_ref, own_ref, one_ref, two_ref, seg_ref, lag_ref, qg_ref, kg_ref, *rest
):
    out_ref, dq_ref, d_own_ref, d_one_ref, d_two_ref, gain_ref, bias, coef = rest[-8:]
    before = rest[:-8]
    tok, wide = q_ref.shape
    width = qg_ref.shape[1]
    heads = wide // width
    scale = width ** (-0.5)

    @pl.when(pl.program_id(0) == 0)
    def _():
        rank = lax.axis_index(axis)

        def seg_block(back):
            start = pl.multiple_of(jnp.maximum(rank - back, 0) * tok, tok)
            row = jnp.broadcast_to(seg_ref[0, :, pl.ds(start, tok)], (tok, tok))
            return jnp.where(rank >= back, row, -1)

        mine = seg_block(0)
        seg_q = mine.T
        row = lax.broadcasted_iota(jnp.int32, (tok, tok), 0)
        col = lax.broadcasted_iota(jnp.int32, (tok, tok), 1)
        bias[:, 0:tok] = jnp.where((mine == seg_q) & (col <= row), 0.0, -1e30)
        bias[:, tok : 2 * tok] = jnp.where(seg_block(1) == seg_q, 0.0, -1e30)
        bias[:, 2 * tok : 3 * tok] = jnp.where(seg_block(2) == seg_q, 0.0, -1e30)
        late = jnp.zeros((tok, tok), jnp.int32)
        for r in range(lag_ref.shape[2]):
            late = jnp.where(seg_q == r, lag_ref[0, 0, r], late)
        coef[...] = 8.0 / (8.0 + late.astype(jnp.float32))
        gain_ref[...] = before[-1][...] if before else jnp.zeros_like(gain_ref)

    def stack(ref):
        return jnp.concatenate(
            [ref[:, h * width : (h + 1) * width].astype(jnp.float32) for h in range(heads)], 0
        )

    def spread(tile):
        return jnp.concatenate([tile] * heads, 0)

    q_gain = qg_ref[...]
    k_gain = kg_ref[...]
    qhat, qr = rms_parts(stack(q_ref))
    qs = (qhat * (q_gain * (scale * LOG2E))).astype(jnp.bfloat16)
    khat, _ = rms_parts(
        jnp.concatenate([ref[0].astype(jnp.float32) for ref in (own_ref, one_ref, two_ref)], 0)
    )
    kn = (khat * k_gain).astype(jnp.bfloat16)
    v = jnp.concatenate([ref[1] for ref in (own_ref, one_ref, two_ref)], 0)
    s = lax.dot_general(qs, kn, LAST, preferred_element_type=jnp.float32)
    p = jnp.exp2(s + spread(bias[...]))
    pb = p.astype(jnp.bfloat16)
    inv = 1.0 / jnp.sum(p, -1, keepdims=True)
    out = jnp.dot(pb, v, preferred_element_type=jnp.float32) * inv
    grad = stack(g_ref) * spread(coef[...]) * inv
    gb = grad.astype(jnp.bfloat16)
    delta = jnp.sum(grad * out, -1, keepdims=True)
    dp = lax.dot_general(gb, v, LAST, preferred_element_type=jnp.float32)
    ds = (p * (dp - delta)).astype(jnp.bfloat16)
    dqn = jnp.dot(ds, kn, preferred_element_type=jnp.float32) * scale
    dk = lax.dot_general(ds, qs, ROWS, preferred_element_type=jnp.float32) * (1.0 / LOG2E)
    dv = lax.dot_general(pb, gb, ROWS, preferred_element_type=jnp.float32)
    gain_ref[...] += jnp.sum(dqn * qhat, 0, keepdims=True)
    up = dqn * q_gain
    dq = qr * (up - qhat * jnp.mean(up * qhat, -1, keepdims=True))
    for h in range(heads):
        at = slice(h * width, (h + 1) * width)
        rows = slice(h * tok, (h + 1) * tok)
        out_ref[:, at] = out[rows].astype(jnp.bfloat16)
        dq_ref[:, at] = dq[rows].astype(jnp.bfloat16)
    for i, ref in enumerate((d_own_ref, d_one_ref, d_two_ref)):
        rows = slice(i * tok, (i + 1) * tok)
        ref[0] = dk[rows].astype(jnp.bfloat16)
        ref[1] = dv[rows].astype(jnp.bfloat16)


def finish_kernel(
    kv_ref, own_ref, one_ref, two_ref, parts_ref, qg_ref, kg_ref, out_ref, q_gain_ref, k_gain_ref
):
    width = kg_ref.shape[1]
    gain = kg_ref[...]
    total_gain = jnp.sum(parts_ref[...], 0, keepdims=True)
    q_gain_ref[...] = total_gain
    k_gain_ref[...] = total_gain * qg_ref[...] / gain
    for h in range(kv_ref.shape[2] // width):
        at = slice(h * width, (h + 1) * width)

        def total(i):
            return (
                own_ref[i, :, at].astype(jnp.float32)
                + one_ref[i, :, at].astype(jnp.float32)
                + two_ref[i, :, at].astype(jnp.float32)
            )

        khat, kr = rms_parts(kv_ref[0, :, at].astype(jnp.float32))
        up = total(0) * gain
        dk = kr * (up - khat * jnp.mean(up * khat, -1, keepdims=True))
        out_ref[0, :, at] = dk.astype(jnp.bfloat16)
        out_ref[1, :, at] = total(1).astype(jnp.bfloat16)


def attention(first, query, grad_out, key_value, one, two, segment_ids, lag, q_gain, k_gain, before):
    tok, wide = query.shape
    width = q_gain.shape[1]
    kv_heads = key_value.shape[2] // width
    number = one.shape[2] // width
    part = wide // kv_heads
    q_spec = pl.BlockSpec((tok, part), lambda g: (0, g + first))
    kv_spec = pl.BlockSpec((2, tok, width), lambda g: (0, 0, g + first))
    halo_spec = pl.BlockSpec((2, tok, width), lambda g: (0, 0, g))
    whole = lambda a: pl.BlockSpec(a.shape, lambda g: (0,) * a.ndim)
    kept = jax.ShapeDtypeStruct(key_value.shape, jnp.bfloat16)
    rows = jax.ShapeDtypeStruct(query.shape, jnp.bfloat16)
    any_spec = pl.BlockSpec(memory_space=pl.ANY)
    vector = pl.BlockSpec((1, width), lambda g: (0, 0))
    operands = (query, grad_out, key_value, one, two, segment_ids, lag, q_gain, k_gain)
    return pl.pallas_call(
        functools.partial(attention_kernel, "sp"),
        grid=(number,),
        in_specs=[
            q_spec, q_spec, kv_spec, halo_spec, halo_spec, whole(segment_ids),
            pl.BlockSpec(memory_space=pltpu.SMEM), whole(q_gain), whole(k_gain),
        ] + ([any_spec] * 5 + [vector] if before else []),
        out_specs=[q_spec, q_spec, kv_spec, kv_spec, kv_spec, vector],
        out_shape=[rows, rows, kept, kept, kept, jax.ShapeDtypeStruct((1, width), jnp.float32)],
        input_output_aliases={len(operands) + i: i for i in range(len(before))},
        scratch_shapes=[
            pltpu.VMEM((tok, 3 * tok), jnp.float32),
            pltpu.VMEM((tok, tok), jnp.float32),
        ],
        compiler_params=pltpu.CompilerParams(vmem_limit_bytes=60 * MIB),
        cost_estimate=pl.CostEstimate(
            flops=36 * tok * tok * part * number, bytes_accessed=8 * tok * part * number,
            transcendentals=3 * tok * tok * part * number // width,
        ),
        name=f"attention{first}",
    )(*operands, *before)


def finish(key_value, own, one, two, parts, q_gain, k_gain):
    vector = jax.ShapeDtypeStruct(k_gain.shape, jnp.float32)
    return pl.pallas_call(
        finish_kernel,
        out_shape=[jax.ShapeDtypeStruct(key_value.shape, jnp.bfloat16), vector, vector],
        compiler_params=pltpu.CompilerParams(vmem_limit_bytes=16 * MIB),
        name="finish",
    )(key_value, own, one, two, parts, q_gain, k_gain)


def local(query, key_value, grad_out, segment_ids, lag, q_gain, k_gain):
    shards = lax.axis_size("sp")
    width = q_gain.shape[0]
    q_gain = q_gain.reshape(1, width)
    k_gain = k_gain.reshape(1, width)

    def shift(x, by):
        return lax.ppermute(x, "sp", [(i, (i + by) % shards) for i in range(shards)])

    one = shift(key_value, 1)
    two = shift(key_value, 2)
    out, d_query, d_own, d_one, d_two, gain = attention(
        0, query, grad_out, key_value, one, two, segment_ids, lag, q_gain, k_gain, ()
    )
    d_one = shift(d_one, -1)
    d_two = shift(d_two, -2)
    gain = gain + lax.ppermute(gain, "core", [(0, 1), (1, 0)])
    chips = ("chip", "sp")
    copies = jnp.broadcast_to(gain, (lax.axis_size(chips), width))
    parts = lax.all_to_all(copies, chips, 0, 0, tiled=True)
    d_key_value, d_q_gain, d_k_gain = finish(
        key_value, d_own, d_one, d_two, parts, q_gain, k_gain
    )
    return out, d_query, d_key_value, d_q_gain.reshape(width), d_k_gain.reshape(width)


def solution(mesh):
    groups, shards = mesh.devices.shape
    mesh = Mesh(mesh.devices.reshape(groups // 2, 2, shards), ("chip", "core", "sp"))
    tokens = P(("chip", "core", "sp"), None)
    pair = P(None, ("chip", "core", "sp"), None)
    group = P(("chip", "core"), None, None)
    return jax.shard_map(
        local,
        mesh=mesh,
        in_specs=(tokens, pair, tokens, group, group, P(), P()),
        out_specs=(tokens, tokens, pair, P(), P()),
        check_vma=False,
    )
```

```python
import functools
import math

import jax
import jax.numpy as jnp
from jax import lax
from jax.experimental import pallas as pl
from jax.experimental.pallas import tpu as pltpu
from jax.sharding import Mesh, PartitionSpec as P

EPS = 1e-06
LOG2E = math.log2(math.e)
ROWS = (((0,), (0,)), ((), ()))
LAST = (((1,), (1,)), ((), ()))
MIB = 2**20


def rms_parts(x):
    inverse = lax.rsqrt(jnp.mean(x * x, -1, keepdims=True) + EPS)
    return x * inverse, inverse


def token_setup(axis, seg_ref, lag_ref, tok):
    rank = lax.axis_index(axis)

    def seg_block(back):
        start = pl.multiple_of(jnp.maximum(rank - back, 0) * tok, tok)
        row = jnp.broadcast_to(seg_ref[0, :, pl.ds(start, tok)], (tok, tok))
        return jnp.where(rank >= back, row, -1)

    seg_q = seg_block(0).T
    late = jnp.zeros((tok, tok), jnp.int32)
    for r in range(lag_ref.shape[2]):
        late = jnp.where(seg_q == r, lag_ref[0, 0, r], late)
    return seg_q, seg_block, 8.0 / (8.0 + late.astype(jnp.float32))


def stack(ref, heads, group, width):
    first = group * heads
    return jnp.concatenate(
        [
            ref[:, h * width : (h + 1) * width].astype(jnp.float32)
            for h in range(first, first + heads)
        ],
        0,
    )


def spread(tile, heads):
    return jnp.concatenate([tile] * heads, 0)


def query_scale(qg_ref):
    return qg_ref[...] * (qg_ref.shape[1] ** (-0.5) * LOG2E)


def own_kernel(
    axis, q_ref, g_ref, own_ref, seg_ref, lag_ref, qg_ref, kg_ref, p_ref, o_ref, dp_ref,
    halo_bias, coef, bias,
):
    tok, wide = q_ref.shape
    heads = wide // qg_ref.shape[1]

    @pl.when(pl.program_id(0) == 0)
    def _():
        seg_q, seg_block, weight = token_setup(axis, seg_ref, lag_ref, tok)
        row = lax.broadcasted_iota(jnp.int32, (tok, tok), 0)
        col = lax.broadcasted_iota(jnp.int32, (tok, tok), 1)
        bias[...] = jnp.where((seg_block(0) == seg_q) & (col <= row), 0.0, -1e30)
        coef[...] = weight
        halo_bias[:, 0:tok] = jnp.where(seg_block(1) == seg_q, 0.0, -1e30)
        halo_bias[:, tok : 2 * tok] = jnp.where(seg_block(2) == seg_q, 0.0, -1e30)

    qhat, _ = rms_parts(stack(q_ref, heads, 0, kg_ref.shape[1]))
    qs = (qhat * query_scale(qg_ref)).astype(jnp.bfloat16)
    khat, _ = rms_parts(own_ref[0].astype(jnp.float32))
    kn = (khat * kg_ref[...]).astype(jnp.bfloat16)
    v = own_ref[1]
    s = lax.dot_general(qs, kn, LAST, preferred_element_type=jnp.float32)
    p = jnp.exp2(s + spread(bias[...], heads)).astype(jnp.bfloat16)
    p_ref[...] = p
    o_ref[...] = jnp.dot(p, v, preferred_element_type=jnp.float32)
    grad = (stack(g_ref, heads, 0, kg_ref.shape[1]) * spread(coef[...], heads)).astype(jnp.bfloat16)
    dp_ref[...] = lax.dot_general(
        grad, v, LAST, preferred_element_type=jnp.float32
    ).astype(jnp.bfloat16)


def attention_kernel(
    q_ref, g_ref, p_ref, o_ref, dp_ref, bias, coef, own_ref, one_ref, two_ref, qg_ref, kg_ref,
    out_ref, dq_ref, d_own_ref, d_one_ref, d_two_ref, gain_ref, out_buf, dq_buf, sems,
):
    tok, wide = q_ref.shape
    width = qg_ref.shape[1]
    kv_heads = own_ref.shape[2] // width
    part = wide // kv_heads
    heads = part // width
    scale = width ** (-0.5)
    q_gain = qg_ref[...]
    gain = jnp.zeros_like(gain_ref)
    copies = []
    for g in range(kv_heads):
        at_kv = slice(g * width, (g + 1) * width)
        stacked = slice(g * heads * tok, (g + 1) * heads * tok)
        qhat, qr = rms_parts(stack(q_ref, heads, g, width))
        qs = (qhat * query_scale(qg_ref)).astype(jnp.bfloat16)
        refs = (own_ref, one_ref, two_ref)
        khat, _ = rms_parts(
            jnp.concatenate([ref[0, :, at_kv].astype(jnp.float32) for ref in refs], 0)
        )
        kn = (khat * kg_ref[...]).astype(jnp.bfloat16)
        v_halo = jnp.concatenate([ref[1, :, at_kv] for ref in refs[1:]], 0)
        s = lax.dot_general(qs, kn[tok:], LAST, preferred_element_type=jnp.float32)
        p = jnp.exp2(s + spread(bias[...], heads))
        pb = p.astype(jnp.bfloat16)
        p_own = p_ref[stacked, :].astype(jnp.float32)
        inv = 1.0 / jnp.sum(p_own + p[:, :tok] + p[:, tok:], -1, keepdims=True)
        halo = jnp.dot(pb, v_halo, preferred_element_type=jnp.float32)
        out = (o_ref[stacked, :] + halo) * inv
        grad = stack(g_ref, heads, g, width) * spread(coef[...], heads) * inv
        gb = grad.astype(jnp.bfloat16)
        delta = jnp.sum(grad * out, -1, keepdims=True)
        dp = lax.dot_general(gb, v_halo, LAST, preferred_element_type=jnp.float32)
        dp_own = dp_ref[stacked, :].astype(jnp.float32)
        ds = jnp.concatenate(
            [
                (p_own * (dp_own * inv - delta)).astype(jnp.bfloat16),
                (p * (dp - delta)).astype(jnp.bfloat16),
            ],
            1,
        )
        dqn = jnp.dot(ds, kn, preferred_element_type=jnp.float32) * scale
        dk = lax.dot_general(ds, qs, ROWS, preferred_element_type=jnp.float32) * (1.0 / LOG2E)
        p_all = jnp.concatenate([p_ref[stacked, :], pb], 1)
        dv = lax.dot_general(gb, p_all, ROWS, preferred_element_type=jnp.float32).T
        gain += jnp.sum(dqn * qhat, 0, keepdims=True)
        up = dqn * q_gain
        dq = qr * (up - qhat * jnp.mean(up * qhat, -1, keepdims=True))
        for h in range(heads):
            at = slice(h * width, (h + 1) * width)
            rows = slice(h * tok, (h + 1) * tok)
            out_buf[g, :, at] = out[rows].astype(jnp.bfloat16)
            dq_buf[g, :, at] = dq[rows].astype(jnp.bfloat16)
        for i, (buf, ref) in enumerate(((out_buf, out_ref), (dq_buf, dq_ref))):
            copy = pltpu.make_async_copy(
                buf.at[g], ref.at[:, pl.ds(g * part, part)], sems.at[g, i]
            )
            copy.start()
            copies.append(copy)
        for i, ref in enumerate((d_own_ref, d_one_ref, d_two_ref)):
            rows = slice(i * tok, (i + 1) * tok)
            ref[0, :, at_kv] = dk[rows].astype(jnp.bfloat16)
            ref[1, :, at_kv] = dv[rows].astype(jnp.bfloat16)
    gain_ref[...] = gain
    for copy in copies:
        copy.wait()


def finish_kernel(
    kv_ref, own_ref, one_ref, two_ref, parts_ref, qg_ref, kg_ref, out_ref, q_gain_ref, k_gain_ref
):
    width = kg_ref.shape[1]
    gain = kg_ref[...]
    total_gain = jnp.sum(parts_ref[...], 0, keepdims=True)
    q_gain_ref[...] = total_gain
    k_gain_ref[...] = total_gain * qg_ref[...] / gain
    for h in range(kv_ref.shape[2] // width):
        at = slice(h * width, (h + 1) * width)

        def total(i):
            return (
                own_ref[i, :, at].astype(jnp.float32)
                + one_ref[i, :, at].astype(jnp.float32)
                + two_ref[i, :, at].astype(jnp.float32)
            )

        khat, kr = rms_parts(kv_ref[0, :, at].astype(jnp.float32))
        up = total(0) * gain
        dk = kr * (up - khat * jnp.mean(up * khat, -1, keepdims=True))
        out_ref[0, :, at] = dk.astype(jnp.bfloat16)
        out_ref[1, :, at] = total(1).astype(jnp.bfloat16)


def attention(query, grad_out, key_value, one, two, segment_ids, lag, q_gain, k_gain):
    tok, wide = query.shape
    width = q_gain.shape[1]
    kv_heads = key_value.shape[2] // width
    part = wide // kv_heads
    stacked = tok * part // width
    q_spec = pl.BlockSpec((tok, part), lambda g: (0, g))
    kv_spec = pl.BlockSpec((2, tok, width), lambda g: (0, 0, g))
    own_spec = pl.BlockSpec((stacked, width), lambda g: (g, 0))
    whole = lambda a: pl.BlockSpec(a.shape, lambda g: (0,) * a.ndim)
    kept = jax.ShapeDtypeStruct(key_value.shape, jnp.bfloat16)
    rows = jax.ShapeDtypeStruct(query.shape, jnp.bfloat16)
    stack_shape = lambda t: jax.ShapeDtypeStruct((kv_heads * stacked, width), t)
    smem = pl.BlockSpec(memory_space=pltpu.SMEM)
    gains = [whole(q_gain), whole(k_gain)]
    mask = lambda n: jax.ShapeDtypeStruct((tok, n * tok), jnp.float32)
    cost = lambda units: pl.CostEstimate(
        flops=2 * units * tok * tok * wide, bytes_accessed=8 * tok * wide,
        transcendentals=2 * tok * tok * wide // width,
    )
    own = pl.pallas_call(
        functools.partial(own_kernel, "sp"),
        grid=(kv_heads,),
        in_specs=[q_spec, q_spec, kv_spec, whole(segment_ids), smem] + gains,
        out_specs=[own_spec] * 3 + [whole(mask(2)), whole(mask(1))],
        out_shape=[
            stack_shape(jnp.bfloat16), stack_shape(jnp.float32), stack_shape(jnp.bfloat16),
            mask(2), mask(1),
        ],
        scratch_shapes=[pltpu.VMEM((tok, tok), jnp.float32)],
        compiler_params=pltpu.CompilerParams(vmem_limit_bytes=24 * MIB),
        cost_estimate=cost(3),
        name="own",
    )(query, grad_out, key_value, segment_ids, lag, q_gain, k_gain)
    vmem = pl.BlockSpec(memory_space=pltpu.VMEM)
    hbm = pl.BlockSpec(memory_space=pl.ANY)
    return pl.pallas_call(
        attention_kernel,
        in_specs=[vmem] * 12,
        out_specs=[hbm, hbm] + [vmem] * 4,
        out_shape=[rows, rows, kept, kept, kept, jax.ShapeDtypeStruct((1, width), jnp.float32)],
        scratch_shapes=[
            pltpu.VMEM((kv_heads, tok, part), jnp.bfloat16),
            pltpu.VMEM((kv_heads, tok, part), jnp.bfloat16),
            pltpu.SemaphoreType.DMA((kv_heads, 2)),
        ],
        compiler_params=pltpu.CompilerParams(vmem_limit_bytes=28 * MIB),
        cost_estimate=cost(15),
        name="attention",
    )(query, grad_out, *own, key_value, one, two, q_gain, k_gain)


def finish(key_value, own, one, two, parts, q_gain, k_gain):
    vector = jax.ShapeDtypeStruct(k_gain.shape, jnp.float32)
    return pl.pallas_call(
        finish_kernel,
        out_shape=[jax.ShapeDtypeStruct(key_value.shape, jnp.bfloat16), vector, vector],
        compiler_params=pltpu.CompilerParams(vmem_limit_bytes=16 * MIB),
        name="finish",
    )(key_value, own, one, two, parts, q_gain, k_gain)


def local(query, key_value, grad_out, segment_ids, lag, q_gain, k_gain):
    shards = lax.axis_size("sp")
    width = q_gain.shape[0]
    q_gain = q_gain.reshape(1, width)
    k_gain = k_gain.reshape(1, width)

    def shift(x, by):
        pairs = {i: i + by for i in range(shards) if 0 <= i + by < shards}
        free = sorted(set(range(shards)) - set(pairs.values()), reverse=True)
        pairs.update(zip(sorted(set(range(shards)) - set(pairs)), free))
        return lax.ppermute(x, "sp", sorted(pairs.items()))

    one = shift(key_value, 1)
    two = shift(key_value, 2)
    out, d_query, d_own, d_one, d_two, gain = attention(
        query, grad_out, key_value, one, two, segment_ids, lag, q_gain, k_gain
    )
    d_one = shift(d_one, -1)
    d_two = shift(d_two, -2)
    gain = gain + lax.ppermute(gain, "core", [(0, 1), (1, 0)])
    chips = ("chip", "sp")
    copies = jnp.broadcast_to(gain, (lax.axis_size(chips), width))
    parts = lax.all_to_all(copies, chips, 0, 0, tiled=True)
    d_key_value, d_q_gain, d_k_gain = finish(
        key_value, d_own, d_one, d_two, parts, q_gain, k_gain
    )
    return out, d_query, d_key_value, d_q_gain.reshape(width), d_k_gain.reshape(width)


def solution(mesh):
    groups, shards = mesh.devices.shape
    mesh = Mesh(mesh.devices.reshape(groups // 2, 2, shards), ("chip", "core", "sp"))
    tokens = P(("chip", "core", "sp"), None)
    pair = P(None, ("chip", "core", "sp"), None)
    group = P(("chip", "core"), None, None)
    return jax.shard_map(
        local,
        mesh=mesh,
        in_specs=(tokens, pair, tokens, group, group, P(), P()),
        out_specs=(tokens, tokens, pair, P(), P()),
        check_vma=False,
    )
```

```python
import functools
import math

import jax
import jax.numpy as jnp
from jax import lax
from jax.experimental import pallas as pl
from jax.experimental.pallas import tpu as pltpu
from jax.sharding import Mesh, PartitionSpec as P

EPS = 1e-06
LOG2E = math.log2(math.e)
ROWS = (((0,), (0,)), ((), ()))
LAST = (((1,), (1,)), ((), ()))
MIB = 2**20


def rms_parts(x):
    inverse = lax.rsqrt(jnp.mean(x * x, -1, keepdims=True) + EPS)
    return x * inverse, inverse


def token_setup(axis, seg_ref, lag_ref, tok):
    rank = lax.axis_index(axis)

    def seg_block(back):
        start = pl.multiple_of(jnp.maximum(rank - back, 0) * tok, tok)
        row = jnp.broadcast_to(seg_ref[0, :, pl.ds(start, tok)], (tok, tok))
        return jnp.where(rank >= back, row, -1)

    seg_q = seg_block(0).T
    late = jnp.zeros((tok, tok), jnp.int32)
    for r in range(lag_ref.shape[2]):
        late = jnp.where(seg_q == r, lag_ref[0, 0, r], late)
    return seg_q, seg_block, 8.0 / (8.0 + late.astype(jnp.float32))


def stack(ref, heads, group, width):
    first = group * heads
    return jnp.concatenate(
        [
            ref[:, h * width : (h + 1) * width].astype(jnp.float32)
            for h in range(first, first + heads)
        ],
        0,
    )


def spread(tile, heads):
    return jnp.concatenate([tile] * heads, 0)


def query_scale(qg_ref):
    return qg_ref[...] * (qg_ref.shape[1] ** (-0.5) * LOG2E)


def own_kernel(
    axis, q_ref, g_ref, own_ref, seg_ref, lag_ref, qg_ref, kg_ref, p_ref, o_ref, dp_ref,
    halo_bias, coef, bias,
):
    tok, wide = q_ref.shape
    heads = wide // qg_ref.shape[1]

    @pl.when(pl.program_id(0) == 0)
    def _():
        seg_q, seg_block, weight = token_setup(axis, seg_ref, lag_ref, tok)
        row = lax.broadcasted_iota(jnp.int32, (tok, tok), 0)
        col = lax.broadcasted_iota(jnp.int32, (tok, tok), 1)
        bias[...] = jnp.where((seg_block(0) == seg_q) & (col <= row), 0.0, -1e30)
        coef[...] = weight
        halo_bias[:, 0:tok] = jnp.where(seg_block(1) == seg_q, 0.0, -1e30)
        halo_bias[:, tok : 2 * tok] = jnp.where(seg_block(2) == seg_q, 0.0, -1e30)

    qhat, _ = rms_parts(stack(q_ref, heads, 0, kg_ref.shape[1]))
    qs = (qhat * query_scale(qg_ref)).astype(jnp.bfloat16)
    khat, _ = rms_parts(own_ref[0].astype(jnp.float32))
    kn = (khat * kg_ref[...]).astype(jnp.bfloat16)
    v = own_ref[1]
    s = lax.dot_general(qs, kn, LAST, preferred_element_type=jnp.float32)
    p = jnp.exp2(s + spread(bias[...], heads)).astype(jnp.bfloat16)
    p_ref[...] = p
    o_ref[...] = jnp.dot(p, v, preferred_element_type=jnp.float32)
    grad = (stack(g_ref, heads, 0, kg_ref.shape[1]) * spread(coef[...], heads)).astype(jnp.bfloat16)
    dp_ref[...] = lax.dot_general(
        grad, v, LAST, preferred_element_type=jnp.float32
    ).astype(jnp.bfloat16)


def attention_kernel(
    q_ref, g_ref, p_ref, o_ref, dp_ref, bias, coef, own_ref, one_ref, two_ref, qg_ref, kg_ref,
    out_ref, dq_ref, d_own_ref, d_one_ref, d_two_ref, gain_ref, out_buf, dq_buf, sems,
):
    tok, wide = q_ref.shape
    width = qg_ref.shape[1]
    kv_heads = own_ref.shape[2] // width
    part = wide // kv_heads
    heads = part // width
    scale = width ** (-0.5)
    q_gain = qg_ref[...]
    copies = []
    gains = []

    def scores(g):
        at_kv = slice(g * width, (g + 1) * width)
        stacked = slice(g * heads * tok, (g + 1) * heads * tok)
        qhat, qr = rms_parts(stack(q_ref, heads, g, width))
        qs = (qhat * query_scale(qg_ref)).astype(jnp.bfloat16)
        refs = (own_ref, one_ref, two_ref)
        khat, _ = rms_parts(
            jnp.concatenate([ref[0, :, at_kv].astype(jnp.float32) for ref in refs], 0)
        )
        kn = (khat * kg_ref[...]).astype(jnp.bfloat16)
        s = lax.dot_general(qs, kn[tok:], LAST, preferred_element_type=jnp.float32)
        p = jnp.exp2(s + spread(bias[...], heads))
        pb = p.astype(jnp.bfloat16)
        p_own = p_ref[stacked, :].astype(jnp.float32)
        inv = 1.0 / jnp.sum(p_own + p[:, :tok] + p[:, tok:], -1, keepdims=True)
        return g, qhat, qr, qs, kn, p, pb, inv

    def weights(g, qhat, qr, qs, kn, p, pb, inv):
        at_kv = slice(g * width, (g + 1) * width)
        stacked = slice(g * heads * tok, (g + 1) * heads * tok)
        v_halo = jnp.concatenate([ref[1, :, at_kv] for ref in (one_ref, two_ref)], 0)
        halo = jnp.dot(pb, v_halo, preferred_element_type=jnp.float32)
        out = (o_ref[stacked, :] + halo) * inv
        grad = stack(g_ref, heads, g, width) * spread(coef[...], heads) * inv
        gb = grad.astype(jnp.bfloat16)
        delta = jnp.sum(grad * out, -1, keepdims=True)
        dp = lax.dot_general(gb, v_halo, LAST, preferred_element_type=jnp.float32)
        p_own = p_ref[stacked, :].astype(jnp.float32)
        dp_own = dp_ref[stacked, :].astype(jnp.float32)
        ds = jnp.concatenate(
            [
                (p_own * (dp_own * inv - delta)).astype(jnp.bfloat16),
                (p * (dp - delta)).astype(jnp.bfloat16),
            ],
            1,
        )
        for h in range(heads):
            rows = slice(h * tok, (h + 1) * tok)
            out_buf[g, :, h * width : (h + 1) * width] = out[rows].astype(jnp.bfloat16)
        return g, qhat, qr, qs, kn, pb, gb, ds

    def gradients(g, qhat, qr, qs, kn, pb, gb, ds):
        at_kv = slice(g * width, (g + 1) * width)
        stacked = slice(g * heads * tok, (g + 1) * heads * tok)
        dqn = jnp.dot(ds, kn, preferred_element_type=jnp.float32) * scale
        dk = lax.dot_general(qs, ds, ROWS, preferred_element_type=jnp.float32).T * (1.0 / LOG2E)
        p_all = jnp.concatenate([p_ref[stacked, :], pb], 1)
        dv = lax.dot_general(gb, p_all, ROWS, preferred_element_type=jnp.float32).T
        gains.append(jnp.sum(dqn * qhat, 0, keepdims=True))
        up = dqn * q_gain
        dq = qr * (up - qhat * jnp.mean(up * qhat, -1, keepdims=True))
        for h in range(heads):
            rows = slice(h * tok, (h + 1) * tok)
            dq_buf[g, :, h * width : (h + 1) * width] = dq[rows].astype(jnp.bfloat16)
        for i, (buf, ref) in enumerate(((out_buf, out_ref), (dq_buf, dq_ref))):
            copy = pltpu.make_async_copy(
                buf.at[g], ref.at[:, pl.ds(g * part, part)], sems.at[g, i]
            )
            copy.start()
            copies.append(copy)
        for i, ref in enumerate((d_own_ref, d_one_ref, d_two_ref)):
            rows = slice(i * tok, (i + 1) * tok)
            ref[0, :, at_kv] = dk[rows].astype(jnp.bfloat16)
            ref[1, :, at_kv] = dv[rows].astype(jnp.bfloat16)

    first, second = {}, {}
    for t in range(kv_heads + 2):
        if t - 2 in second:
            gradients(*second[t - 2])
        if t - 1 in first:
            second[t - 1] = weights(*first[t - 1])
        if t < kv_heads:
            first[t] = scores(t)
    gain = sum(gains[1:], gains[0])
    gain_ref[...] = gain
    for copy in copies:
        copy.wait()


def finish_kernel(
    kv_ref, own_ref, one_ref, two_ref, parts_ref, qg_ref, kg_ref, out_ref, q_gain_ref, k_gain_ref
):
    width = kg_ref.shape[1]
    gain = kg_ref[...]
    total_gain = jnp.sum(parts_ref[...], 0, keepdims=True)
    q_gain_ref[...] = total_gain
    k_gain_ref[...] = total_gain * qg_ref[...] / gain
    for h in range(kv_ref.shape[2] // width):
        at = slice(h * width, (h + 1) * width)

        def total(i):
            return (
                own_ref[i, :, at].astype(jnp.float32)
                + one_ref[i, :, at].astype(jnp.float32)
                + two_ref[i, :, at].astype(jnp.float32)
            )

        khat, kr = rms_parts(kv_ref[0, :, at].astype(jnp.float32))
        up = total(0) * gain
        dk = kr * (up - khat * jnp.mean(up * khat, -1, keepdims=True))
        out_ref[0, :, at] = dk.astype(jnp.bfloat16)
        out_ref[1, :, at] = total(1).astype(jnp.bfloat16)


def attention(query, grad_out, key_value, one, two, segment_ids, lag, q_gain, k_gain):
    tok, wide = query.shape
    width = q_gain.shape[1]
    kv_heads = key_value.shape[2] // width
    part = wide // kv_heads
    stacked = tok * part // width
    q_spec = pl.BlockSpec((tok, part), lambda g: (0, g))
    kv_spec = pl.BlockSpec((2, tok, width), lambda g: (0, 0, g))
    own_spec = pl.BlockSpec((stacked, width), lambda g: (g, 0))
    whole = lambda a: pl.BlockSpec(a.shape, lambda g: (0,) * a.ndim)
    kept = jax.ShapeDtypeStruct(key_value.shape, jnp.bfloat16)
    rows = jax.ShapeDtypeStruct(query.shape, jnp.bfloat16)
    stack_shape = lambda t: jax.ShapeDtypeStruct((kv_heads * stacked, width), t)
    smem = pl.BlockSpec(memory_space=pltpu.SMEM)
    gains = [whole(q_gain), whole(k_gain)]
    mask = lambda n: jax.ShapeDtypeStruct((tok, n * tok), jnp.float32)
    cost = lambda units: pl.CostEstimate(
        flops=2 * units * tok * tok * wide, bytes_accessed=8 * tok * wide,
        transcendentals=2 * tok * tok * wide // width,
    )
    own = pl.pallas_call(
        functools.partial(own_kernel, "sp"),
        grid=(kv_heads,),
        in_specs=[q_spec, q_spec, kv_spec, whole(segment_ids), smem] + gains,
        out_specs=[own_spec] * 3 + [whole(mask(2)), whole(mask(1))],
        out_shape=[
            stack_shape(jnp.bfloat16), stack_shape(jnp.float32), stack_shape(jnp.bfloat16),
            mask(2), mask(1),
        ],
        scratch_shapes=[pltpu.VMEM((tok, tok), jnp.float32)],
        compiler_params=pltpu.CompilerParams(vmem_limit_bytes=24 * MIB),
        cost_estimate=cost(3),
        name="own",
    )(query, grad_out, key_value, segment_ids, lag, q_gain, k_gain)
    vmem = pl.BlockSpec(memory_space=pltpu.VMEM)
    hbm = pl.BlockSpec(memory_space=pl.ANY)
    return pl.pallas_call(
        attention_kernel,
        in_specs=[vmem] * 12,
        out_specs=[hbm, hbm] + [vmem] * 4,
        out_shape=[rows, rows, kept, kept, kept, jax.ShapeDtypeStruct((1, width), jnp.float32)],
        scratch_shapes=[
            pltpu.VMEM((kv_heads, tok, part), jnp.bfloat16),
            pltpu.VMEM((kv_heads, tok, part), jnp.bfloat16),
            pltpu.SemaphoreType.DMA((kv_heads, 2)),
        ],
        compiler_params=pltpu.CompilerParams(vmem_limit_bytes=28 * MIB),
        cost_estimate=cost(15),
        name="attention",
    )(query, grad_out, *own, key_value, one, two, q_gain, k_gain)


def finish(key_value, own, one, two, parts, q_gain, k_gain):
    vector = jax.ShapeDtypeStruct(k_gain.shape, jnp.float32)
    return pl.pallas_call(
        finish_kernel,
        out_shape=[jax.ShapeDtypeStruct(key_value.shape, jnp.bfloat16), vector, vector],
        compiler_params=pltpu.CompilerParams(vmem_limit_bytes=16 * MIB),
        name="finish",
    )(key_value, own, one, two, parts, q_gain, k_gain)


def local(query, key_value, grad_out, segment_ids, lag, q_gain, k_gain):
    shards = lax.axis_size("sp")
    width = q_gain.shape[0]
    q_gain = q_gain.reshape(1, width)
    k_gain = k_gain.reshape(1, width)

    def shift(x, by):
        pairs = {i: i + by for i in range(shards) if 0 <= i + by < shards}
        free = sorted(set(range(shards)) - set(pairs.values()), reverse=True)
        pairs.update(zip(sorted(set(range(shards)) - set(pairs)), free))
        return lax.ppermute(x, "sp", sorted(pairs.items()))

    one = shift(key_value, 1)
    two = shift(key_value, 2)
    out, d_query, d_own, d_one, d_two, gain = attention(
        query, grad_out, key_value, one, two, segment_ids, lag, q_gain, k_gain
    )
    d_one = shift(d_one, -1)
    d_two = shift(d_two, -2)
    gain = gain + lax.ppermute(gain, "core", [(0, 1), (1, 0)])
    chips = ("chip", "sp")
    copies = jnp.broadcast_to(gain, (lax.axis_size(chips), width))
    parts = lax.all_to_all(copies, chips, 0, 0, tiled=True)
    d_key_value, d_q_gain, d_k_gain = finish(
        key_value, d_own, d_two, d_one, parts, q_gain, k_gain
    )
    return out, d_query, d_key_value, d_q_gain.reshape(width), d_k_gain.reshape(width)


def solution(mesh):
    groups, shards = mesh.devices.shape
    mesh = Mesh(mesh.devices.reshape(groups // 2, 2, shards), ("chip", "core", "sp"))
    tokens = P(("chip", "core", "sp"), None)
    pair = P(None, ("chip", "core", "sp"), None)
    group = P(("chip", "core"), None, None)
    return jax.shard_map(
        local,
        mesh=mesh,
        in_specs=(tokens, pair, tokens, group, group, P(), P()),
        out_specs=(tokens, tokens, pair, P(), P()),
        check_vma=False,
    )
```

```python
import functools
import math

import jax
import jax.numpy as jnp
from jax import lax
from jax.experimental import pallas as pl
from jax.experimental.pallas import tpu as pltpu
from jax.sharding import Mesh, PartitionSpec as P

EPS = 1e-06
LOG2E = math.log2(math.e)
ROWS = (((0,), (0,)), ((), ()))
LAST = (((1,), (1,)), ((), ()))
MIB = 2**20


def rms_parts(x):
    inverse = lax.rsqrt(jnp.mean(x * x, -1, keepdims=True) + EPS)
    return x * inverse, inverse


def token_setup(axis, seg_ref, lag_ref, tok):
    rank = lax.axis_index(axis)

    def seg_block(back):
        start = pl.multiple_of(jnp.maximum(rank - back, 0) * tok, tok)
        row = jnp.broadcast_to(seg_ref[0, :, pl.ds(start, tok)], (tok, tok))
        return jnp.where(rank >= back, row, -1)

    seg_q = seg_block(0).T
    late = jnp.zeros((tok, tok), jnp.int32)
    for r in range(lag_ref.shape[2]):
        late = jnp.where(seg_q == r, lag_ref[0, 0, r], late)
    return seg_q, seg_block, 8.0 / (8.0 + late.astype(jnp.float32))


def stack(ref, heads, group, width):
    first = group * heads
    return jnp.concatenate(
        [
            ref[:, h * width : (h + 1) * width].astype(jnp.float32)
            for h in range(first, first + heads)
        ],
        0,
    )


def spread(tile, heads):
    return jnp.concatenate([tile] * heads, 0)


def query_scale(qg_ref):
    return qg_ref[...] * (qg_ref.shape[1] ** (-0.5) * LOG2E)


def own_kernel(
    axis, q_ref, g_ref, own_ref, seg_ref, lag_ref, qg_ref, kg_ref, p_ref, o_ref, dp_ref,
    halo_bias, coef, bias,
):
    tok, wide = q_ref.shape
    heads = wide // qg_ref.shape[1]

    @pl.when(pl.program_id(0) == 0)
    def _():
        seg_q, seg_block, weight = token_setup(axis, seg_ref, lag_ref, tok)
        row = lax.broadcasted_iota(jnp.int32, (tok, tok), 0)
        col = lax.broadcasted_iota(jnp.int32, (tok, tok), 1)
        bias[...] = jnp.where((seg_block(0) == seg_q) & (col <= row), 0.0, -1e30)
        coef[...] = weight
        halo_bias[:, 0:tok] = jnp.where(seg_block(1) == seg_q, 0.0, -1e30)
        halo_bias[:, tok : 2 * tok] = jnp.where(seg_block(2) == seg_q, 0.0, -1e30)

    qhat, _ = rms_parts(stack(q_ref, heads, 0, kg_ref.shape[1]))
    qs = (qhat * query_scale(qg_ref)).astype(jnp.bfloat16)
    khat, _ = rms_parts(own_ref[0].astype(jnp.float32))
    kn = (khat * kg_ref[...]).astype(jnp.bfloat16)
    v = own_ref[1]
    s = lax.dot_general(qs, kn, LAST, preferred_element_type=jnp.float32)
    p = jnp.exp2(s + spread(bias[...], heads)).astype(jnp.bfloat16)
    p_ref[...] = p
    o_ref[...] = jnp.dot(p, v, preferred_element_type=jnp.float32)
    grad = (stack(g_ref, heads, 0, kg_ref.shape[1]) * spread(coef[...], heads)).astype(jnp.bfloat16)
    dp_ref[...] = lax.dot_general(
        grad, v, LAST, preferred_element_type=jnp.float32
    ).astype(jnp.bfloat16)


def attention_kernel(
    q_ref, g_ref, p_ref, o_ref, dp_ref, bias, coef, own_ref, one_ref, two_ref, qg_ref, kg_ref,
    out_ref, dq_ref, d_own_ref, d_one_ref, d_two_ref, gain_ref, out_buf, dq_buf, sems,
):
    tok, wide = q_ref.shape
    width = qg_ref.shape[1]
    kv_heads = own_ref.shape[2] // width
    part = wide // kv_heads
    heads = part // width
    scale = width ** (-0.5)
    q_gain = qg_ref[...]
    copies = []
    gains = []

    def scores(g):
        at_kv = slice(g * width, (g + 1) * width)
        stacked = slice(g * heads * tok, (g + 1) * heads * tok)
        qhat, qr = rms_parts(stack(q_ref, heads, g, width))
        qs = (qhat * query_scale(qg_ref)).astype(jnp.bfloat16)
        refs = (own_ref, one_ref, two_ref)
        khat, _ = rms_parts(
            jnp.concatenate([ref[0, :, at_kv].astype(jnp.float32) for ref in refs], 0)
        )
        kn = (khat * kg_ref[...]).astype(jnp.bfloat16)
        s = lax.dot_general(qs, kn[tok:], LAST, preferred_element_type=jnp.float32)
        p = jnp.exp2(s + spread(bias[...], heads))
        pb = p.astype(jnp.bfloat16)
        p_own = p_ref[stacked, :].astype(jnp.float32)
        inv = 1.0 / jnp.sum(p_own + p[:, :tok] + p[:, tok:], -1, keepdims=True)
        return g, qhat, qr, qs, kn, p, pb, inv

    def weights(g, qhat, qr, qs, kn, p, pb, inv):
        at_kv = slice(g * width, (g + 1) * width)
        stacked = slice(g * heads * tok, (g + 1) * heads * tok)
        v_halo = jnp.concatenate([ref[1, :, at_kv] for ref in (one_ref, two_ref)], 0)
        halo = jnp.dot(pb, v_halo, preferred_element_type=jnp.float32)
        out = (o_ref[stacked, :] + halo) * inv
        grad = stack(g_ref, heads, g, width) * spread(coef[...], heads) * inv
        gb = grad.astype(jnp.bfloat16)
        delta = jnp.sum(grad * out, -1, keepdims=True)
        dp = lax.dot_general(gb, v_halo, LAST, preferred_element_type=jnp.float32)
        p_own = p_ref[stacked, :].astype(jnp.float32)
        dp_own = dp_ref[stacked, :].astype(jnp.float32)
        ds = jnp.concatenate(
            [
                (p_own * (dp_own * inv - delta)).astype(jnp.bfloat16),
                (p * (dp - delta)).astype(jnp.bfloat16),
            ],
            1,
        )
        for h in range(heads):
            rows = slice(h * tok, (h + 1) * tok)
            out_buf[g, :, h * width : (h + 1) * width] = out[rows].astype(jnp.bfloat16)
        return g, qhat, qr, qs, kn, pb, gb, ds

    def gradients(g, qhat, qr, qs, kn, pb, gb, ds):
        at_kv = slice(g * width, (g + 1) * width)
        stacked = slice(g * heads * tok, (g + 1) * heads * tok)
        up = jnp.dot(ds, kn, preferred_element_type=jnp.float32) * (q_gain * scale)
        dk = lax.dot_general(qs, ds, ROWS, preferred_element_type=jnp.float32).T * (1.0 / LOG2E)
        p_all = jnp.concatenate([p_ref[stacked, :], pb], 1)
        dv = lax.dot_general(gb, p_all, ROWS, preferred_element_type=jnp.float32).T
        both = up * qhat
        gains.append(jnp.sum(both, 0, keepdims=True))
        dq = qr * (up - qhat * jnp.mean(both, -1, keepdims=True))
        for h in range(heads):
            rows = slice(h * tok, (h + 1) * tok)
            dq_buf[g, :, h * width : (h + 1) * width] = dq[rows].astype(jnp.bfloat16)
        for i, (buf, ref) in enumerate(((out_buf, out_ref), (dq_buf, dq_ref))):
            copy = pltpu.make_async_copy(
                buf.at[g], ref.at[:, pl.ds(g * part, part)], sems.at[g, i]
            )
            copy.start()
            copies.append(copy)
        for i, ref in enumerate((d_own_ref, d_one_ref, d_two_ref)):
            rows = slice(i * tok, (i + 1) * tok)
            ref[0, :, at_kv] = dk[rows].astype(jnp.bfloat16)
            ref[1, :, at_kv] = dv[rows].astype(jnp.bfloat16)

    first, second = {}, {}
    for t in range(kv_heads + 2):
        if t - 2 in second:
            gradients(*second[t - 2])
        if t - 1 in first:
            second[t - 1] = weights(*first[t - 1])
        if t < kv_heads:
            first[t] = scores(t)
    gain = sum(gains[1:], gains[0])
    gain_ref[...] = gain
    for copy in copies:
        copy.wait()


def finish_kernel(
    kv_ref, own_ref, one_ref, two_ref, parts_ref, qg_ref, kg_ref, out_ref, q_gain_ref, k_gain_ref
):
    width = kg_ref.shape[1]
    gain = kg_ref[...]
    total_gain = jnp.sum(parts_ref[...], 0, keepdims=True)
    q_gain_ref[...] = total_gain / qg_ref[...]
    k_gain_ref[...] = total_gain / gain
    for h in range(kv_ref.shape[2] // width):
        at = slice(h * width, (h + 1) * width)

        def total(i):
            return (
                own_ref[i, :, at].astype(jnp.float32)
                + one_ref[i, :, at].astype(jnp.float32)
                + two_ref[i, :, at].astype(jnp.float32)
            )

        khat, kr = rms_parts(kv_ref[0, :, at].astype(jnp.float32))
        up = total(0) * gain
        dk = kr * (up - khat * jnp.mean(up * khat, -1, keepdims=True))
        out_ref[0, :, at] = dk.astype(jnp.bfloat16)
        out_ref[1, :, at] = total(1).astype(jnp.bfloat16)


def attention(query, grad_out, key_value, one, two, segment_ids, lag, q_gain, k_gain):
    tok, wide = query.shape
    width = q_gain.shape[1]
    kv_heads = key_value.shape[2] // width
    part = wide // kv_heads
    stacked = tok * part // width
    q_spec = pl.BlockSpec((tok, part), lambda g: (0, g))
    kv_spec = pl.BlockSpec((2, tok, width), lambda g: (0, 0, g))
    own_spec = pl.BlockSpec((stacked, width), lambda g: (g, 0))
    whole = lambda a: pl.BlockSpec(a.shape, lambda g: (0,) * a.ndim)
    kept = jax.ShapeDtypeStruct(key_value.shape, jnp.bfloat16)
    rows = jax.ShapeDtypeStruct(query.shape, jnp.bfloat16)
    stack_shape = lambda t: jax.ShapeDtypeStruct((kv_heads * stacked, width), t)
    smem = pl.BlockSpec(memory_space=pltpu.SMEM)
    gains = [whole(q_gain), whole(k_gain)]
    mask = lambda n: jax.ShapeDtypeStruct((tok, n * tok), jnp.float32)
    cost = lambda units: pl.CostEstimate(
        flops=2 * units * tok * tok * wide, bytes_accessed=8 * tok * wide,
        transcendentals=2 * tok * tok * wide // width,
    )
    own = pl.pallas_call(
        functools.partial(own_kernel, "sp"),
        grid=(kv_heads,),
        in_specs=[q_spec, q_spec, kv_spec, whole(segment_ids), smem] + gains,
        out_specs=[own_spec] * 3 + [whole(mask(2)), whole(mask(1))],
        out_shape=[
            stack_shape(jnp.bfloat16), stack_shape(jnp.float32), stack_shape(jnp.bfloat16),
            mask(2), mask(1),
        ],
        scratch_shapes=[pltpu.VMEM((tok, tok), jnp.float32)],
        compiler_params=pltpu.CompilerParams(vmem_limit_bytes=24 * MIB),
        cost_estimate=cost(3),
        name="own",
    )(query, grad_out, key_value, segment_ids, lag, q_gain, k_gain)
    vmem = pl.BlockSpec(memory_space=pltpu.VMEM)
    hbm = pl.BlockSpec(memory_space=pl.ANY)
    return pl.pallas_call(
        attention_kernel,
        in_specs=[vmem] * 12,
        out_specs=[hbm, hbm] + [vmem] * 4,
        out_shape=[rows, rows, kept, kept, kept, jax.ShapeDtypeStruct((1, width), jnp.float32)],
        scratch_shapes=[
            pltpu.VMEM((kv_heads, tok, part), jnp.bfloat16),
            pltpu.VMEM((kv_heads, tok, part), jnp.bfloat16),
            pltpu.SemaphoreType.DMA((kv_heads, 2)),
        ],
        compiler_params=pltpu.CompilerParams(vmem_limit_bytes=28 * MIB),
        cost_estimate=cost(15),
        name="attention",
    )(query, grad_out, *own, key_value, one, two, q_gain, k_gain)


def finish(key_value, own, one, two, parts, q_gain, k_gain):
    vector = jax.ShapeDtypeStruct(k_gain.shape, jnp.float32)
    return pl.pallas_call(
        finish_kernel,
        out_shape=[jax.ShapeDtypeStruct(key_value.shape, jnp.bfloat16), vector, vector],
        compiler_params=pltpu.CompilerParams(vmem_limit_bytes=16 * MIB),
        name="finish",
    )(key_value, own, one, two, parts, q_gain, k_gain)


def local(query, key_value, grad_out, segment_ids, lag, q_gain, k_gain):
    shards = lax.axis_size("sp")
    width = q_gain.shape[0]
    q_gain = q_gain.reshape(1, width)
    k_gain = k_gain.reshape(1, width)

    def shift(x, by):
        pairs = {i: i + by for i in range(shards) if 0 <= i + by < shards}
        free = sorted(set(range(shards)) - set(pairs.values()), reverse=True)
        pairs.update(zip(sorted(set(range(shards)) - set(pairs)), free))
        return lax.ppermute(x, "sp", sorted(pairs.items()))

    one = shift(key_value, 1)
    two = shift(key_value, 2)
    out, d_query, d_own, d_one, d_two, gain = attention(
        query, grad_out, key_value, one, two, segment_ids, lag, q_gain, k_gain
    )
    d_one = shift(d_one, -1)
    d_two = shift(d_two, -2)
    gain = gain + lax.ppermute(gain, "core", [(0, 1), (1, 0)])
    chips = ("chip", "sp")
    copies = jnp.broadcast_to(gain, (lax.axis_size(chips), width))
    parts = lax.all_to_all(copies, chips, 0, 0, tiled=True)
    d_key_value, d_q_gain, d_k_gain = finish(
        key_value, d_own, d_two, d_one, parts, q_gain, k_gain
    )
    return out, d_query, d_key_value, d_q_gain.reshape(width), d_k_gain.reshape(width)


def solution(mesh):
    groups, shards = mesh.devices.shape
    mesh = Mesh(mesh.devices.reshape(groups // 2, 2, shards), ("chip", "core", "sp"))
    tokens = P(("chip", "core", "sp"), None)
    pair = P(None, ("chip", "core", "sp"), None)
    group = P(("chip", "core"), None, None)
    return jax.shard_map(
        local,
        mesh=mesh,
        in_specs=(tokens, pair, tokens, group, group, P(), P()),
        out_specs=(tokens, tokens, pair, P(), P()),
        check_vma=False,
    )
```
